256 devices in a mesh: fsdp: 2 (over core), ctx: 128 (over z, x, y).
Axes of the slice: x: 4, y: 4, z: 8, core: 2. Of those that a mesh axis runs over, the one named last changes fastest.
Arguments:
- tokens: bfloat16 [2, 65536, 2048], P('fsdp', 'ctx'), may hold values from -6 to 6
- w_qkv: bfloat16 [2048, 3, 1024], P(None, None, 'fsdp'), may hold values from -0.125 to 0.125
- w_out: bfloat16 [1024, 2048], P('fsdp'), may hold values from -0.1875 to 0.1875
- gain: float32 [1024], replicated, may hold values from 0.1 to 1.9
Outputs:
- mixed: bfloat16 [2, 65536, 2048], P('fsdp', 'ctx')
The draws below stay inside these ranges and needn't reach their ends.
All inputs are finite; a program needn't handle non-finite values.
Results may differ from the reference program's by a relative error of at most 0.007.
Values may be sent and summed in bfloat16 or wider, within the bound.
A program may use at most 192 MiB of HBM per device.

```python
import math
import jax
import jax.numpy as jnp
from jax import lax

D = 2048
HEADS = 8
HD = 128
TOK_DEV = 512
LEN = 65536
HH = 1024
N_FSDP = 2
N_CTX = 128


def draw_tokens(key, part):
    num_blocks = LEN // TOK_DEV
    base_key = jax.random.fold_in(key, 11)
    key_noise, key_rough, key_freq, key_phase = jax.random.split(base_key, 4)
    tok_noise = jax.random.normal(key_noise, (N_FSDP, num_blocks, TOK_DEV, D), jnp.float32)
    amplitude = 0.6
    rough_mean = jax.random.normal(key_rough, (N_FSDP, num_blocks, 1, D), jnp.float32)
    frequency = jax.random.uniform(key_freq, (1, 1, 1, D), jnp.float32, 0.5, 3.0)
    phase_shift = jax.random.uniform(key_phase, (1, 1, 1, D), jnp.float32, -math.pi, math.pi)
    position = jnp.arange(num_blocks, dtype=jnp.float32).reshape(1, num_blocks, 1, 1) / num_blocks
    drift_mean = jnp.sin(2.0 * math.pi * frequency * position + phase_shift)
    seq_sign = jnp.where(jnp.arange(N_FSDP) % 2 == 0, 1.0, -1.0).astype(jnp.float32).reshape(N_FSDP, 1, 1, 1)
    block_mean = seq_sign * (amplitude * rough_mean + amplitude * drift_mean)
    shifted = jnp.clip(tok_noise + block_mean, -6.0, 6.0)
    return shifted.reshape(N_FSDP, LEN, D).astype(jnp.bfloat16)


def shard_levels(own_key, shape, shards, low, high):
    def one(dim, blocks):
        draws = jax.random.uniform(jax.random.fold_in(jax.random.fold_in(own_key, 6), dim), (blocks,), jnp.float32, low / len(shards), high / len(shards))
        return jnp.repeat(jnp.exp(draws), shape[dim] // blocks).reshape((-1,) + (1,) * (len(shape) - dim - 1))

    loudness = one(*shards[0])
    for cut in shards[1:]:
        loudness = loudness * one(*cut)
    return loudness


def noise(rng, extent, scale, bound, shards=(), kind=jnp.bfloat16):
    loudness = shard_levels(rng, extent, shards, -0.22, 0.18) if shards else 1.0
    array = jax.random.normal(rng, extent, jnp.float32) * scale * loudness
    return jnp.minimum(jnp.maximum(array, -bound), bound).astype(kind)


def setup_inputs(seed: int = 0) -> dict:
    seeds = jax.random.split(jax.random.key(seed), 5)
    return {
        "tokens": draw_tokens(jax.random.fold_in(seeds[4], 71), 0),
        "w_qkv": noise(seeds[1], (D, 3, HH), D ** -0.5, 0.125, ((2, 2),)),
        "w_out": noise(seeds[2], (HH, D), HH ** -0.5, 0.1875, ((0, 2),)),
        "gain": jnp.clip(1.0 + 0.18 * jax.random.normal(seeds[3], (HH,), jnp.float32), 0.1, 1.9),
    }


def one_sequence(xseq, w_qkv, w_out, gain):
    blocks = xseq.reshape(N_CTX, TOK_DEV, D)
    w_flat = w_qkv.reshape(D, 3 * HH)
    gain_heads = gain.reshape(HEADS, HD)
    tok_idx = jnp.arange(TOK_DEV, dtype=jnp.int32)
    causal = tok_idx[:, None] >= tok_idx[None, :]

    def step(state, xb):
        qkv = jax.nn.silu(jnp.dot(xb, w_flat, preferred_element_type=jnp.float32)).astype(jnp.bfloat16)
        qkv = qkv.reshape(TOK_DEV, 3, HEADS, HD).astype(jnp.float32)
        query, key_rows, value_rows = (qkv[:, 0], qkv[:, 1], qkv[:, 2])
        kv_block = jnp.einsum('the,thf->hef', key_rows, value_rows, precision=lax.Precision.HIGHEST)
        inter = jnp.einsum('the,hef->thf', query, state, precision=lax.Precision.HIGHEST)
        scores = jnp.einsum('the,she->hts', query, key_rows, precision=lax.Precision.HIGHEST)
        scores = jnp.where(causal[None], scores, 0.0).astype(jnp.bfloat16).astype(jnp.float32)
        intra = jnp.einsum('hts,shf->thf', scores, value_rows, precision=lax.Precision.HIGHEST)
        total = inter + intra
        normed = total * lax.rsqrt(lax.optimization_barrier(jnp.mean(total * total, axis=-1, keepdims=True)) + 1e-06) * gain_heads
        normed = normed.astype(jnp.bfloat16).reshape(TOK_DEV, HH)
        mixed = jnp.dot(normed, w_out, preferred_element_type=jnp.float32).astype(jnp.bfloat16)
        return (state + kv_block, mixed)
    init = jnp.zeros((HEADS, HD, HD), jnp.float32)
    final_state, outs = lax.scan(step, init, blocks)
    return outs.reshape(LEN, D)

def reference(tokens, w_qkv, w_out, gain):
    results = [one_sequence(tokens[seq_index], w_qkv, w_out, gain) for seq_index in range(N_FSDP)]
    return jnp.stack(results, axis=0)
```

```python
import jax
import jax.numpy as jnp
from jax import lax
from jax.experimental import pallas as pl
from jax.experimental.pallas import tpu as pltpu
from jax.sharding import PartitionSpec as P

HD = 128
T = 512
D = 2048
NH = 4
HC = NH * HD
PLANE = 16
NZ = 8
SL = HC // PLANE
F32 = jnp.float32
BF16 = jnp.bfloat16
MESH = pl.DeviceIdType.MESH


def silu(v):
    half = 0.5 * v
    return half + half * jnp.tanh(half)


def remote(src, dst, send, recv, device):
    return pltpu.make_async_remote_copy(
        src_ref=src, dst_ref=dst, send_sem=send, recv_sem=recv, device_id=device, device_id_type=MESH
    )


def kernel(
    x_hbm, w_hbm, wo_hbm, gain_ref, out_hbm,
    x_own, x_oth, w, wo_own, wo_oth,
    qkv_a, qkv_s, qkv_r,
    kv_a, kv_b, r1a, r1b, t2a, t2b, r2a, r2b, o3a, o3b, pfa, pfb,
    y_a, y_b, n_a, n_b, acc, out_v,
    ld_sem, st_sem, ps_sem, pr_sem, s1_sem, q1_sem, s2_sem, q2_sem, s3_sem, q3_sem,
):
    f = lax.axis_index("fsdp")
    c = lax.axis_index("ctx")
    z = c // PLANE
    p = lax.rem(c, PLANE)
    base = z * PLANE
    g = 1 - f

    def chip(k):
        return lax.rem(p + k, PLANE)

    barrier = pltpu.get_barrier_semaphore()
    for k in range(PLANE):
        pl.semaphore_signal(barrier, inc=1, device_id=(g, base + chip(k)), device_id_type=MESH)
        if k:
            pl.semaphore_signal(barrier, inc=1, device_id=(f, base + chip(k)), device_id_type=MESH)
    for k in range(1, NZ):
        pl.semaphore_signal(
            barrier, inc=1, device_id=(f, lax.rem(z + k, NZ) * PLANE + p), device_id_type=MESH
        )

    loads = [pltpu.make_async_copy(x_hbm.at[0], x_own, ld_sem.at[0])]
    for n, which in enumerate((1, 2, 0)):
        loads.append(pltpu.make_async_copy(w_hbm.at[which], w.at[which], ld_sem.at[1 + n]))
    loads.append(pltpu.make_async_copy(wo_hbm, wo_own, ld_sem.at[4]))
    for copy in loads:
        copy.start()

    pl.semaphore_wait(barrier, 2 * PLANE - 1 + NZ - 1)

    partner = (g, c)
    send_x = remote(x_hbm.at[0], x_oth, ps_sem.at[0], pr_sem.at[0], partner)
    send_wo = remote(wo_hbm, wo_oth, ps_sem.at[1], pr_sem.at[1], partner)
    send_k = remote(
        qkv_s.at[:, pl.ds(HC, 2 * HC)], qkv_r.at[:, pl.ds(HC, 2 * HC)], ps_sem.at[2], pr_sem.at[2], partner
    )
    send_q = remote(qkv_s.at[:, pl.ds(0, HC)], qkv_r.at[:, pl.ds(0, HC)], ps_sem.at[3], pr_sem.at[3], partner)

    send_x.start()

    def project(x, which, dst):
        @pl.loop(0, 2)
        def _(i):
            cols = pl.ds(pl.multiple_of(i * 256, 256), 256)
            dcols = pl.ds(pl.multiple_of(which * HC + i * 256, 256), 256)
            part = jnp.dot(x[...], w[which, :, cols], preferred_element_type=F32)
            dst[:, dcols] = silu(part).astype(BF16)

    def state(qkv, dst):
        for h in range(NH):
            key = qkv[:, pl.ds(HC + h * HD, HD)]
            val = qkv[:, pl.ds(2 * HC + h * HD, HD)]
            kv = lax.dot_general(key, val, (((0,), (0,)), ((), ())), preferred_element_type=F32)
            dst[pl.ds(h * HD, HD), :] = kv.astype(BF16)

    def rows(i):
        return pl.ds(pl.multiple_of(i * SL, SL), SL)

    def scatter_start(kv, got, core, n, first):
        for k in range(first, PLANE):
            j = chip(k)
            remote(kv.at[rows(j)], got.at[p], s1_sem.at[n], q1_sem.at[n], (core, base + j)).start()

    def scatter_wait(kv, got, n, first):
        m = PLANE - first
        remote(kv.at[pl.ds(0, m * SL)], kv.at[pl.ds(0, m * SL)], s1_sem.at[n], q1_sem.at[n], partner).wait_recv()

    def totals_start(got, tot, r2, n):
        total = got[0].astype(F32)
        for i in range(1, PLANE):
            total = total + got[i].astype(F32)
        tot[...] = total.astype(BF16)
        for k in range(1, NZ):
            @pl.when(z + k < NZ)
            def _():
                remote(
                    tot, r2.at[z], s2_sem.at[n, k], q2_sem.at[n, z], (f, (z + k) * PLANE + p)
                ).start()

    def prefix_start(got, tot, r2, o3, pf, n):
        def add(i, total):
            remote(tot, r2.at[i], s2_sem.at[n, 0], q2_sem.at[n, i], partner).wait_recv()
            return total + r2[i].astype(F32)

        total = lax.fori_loop(0, z, add, jnp.zeros((SL, HD), F32))
        for i in range(PLANE):
            o3[i] = total.astype(BF16)
            if i < PLANE - 1:
                total = total + got[i].astype(F32)
        for k in range(1, PLANE):
            j = chip(k)
            remote(o3.at[j], pf.at[rows(p)], s3_sem.at[n], q3_sem.at[n], (f, base + j)).start()
        pf[rows(p), :] = o3[p]

    def prefix_wait(pf, n):
        m = PLANE - 1
        remote(pf.at[pl.ds(0, m * SL)], pf.at[pl.ds(0, m * SL)], s3_sem.at[n], q3_sem.at[n], partner).wait_recv()

    half = T // 2
    tri = lax.broadcasted_iota(jnp.int32, (half, half), 0) >= lax.broadcasted_iota(jnp.int32, (half, half), 1)

    def intra(qkv, y):
        nt = (((1,), (1,)), ((), ()))
        for h in range(NH):
            qc, kc, vc = (pl.ds(n * HC + h * HD, HD) for n in range(3))
            lo, hi = pl.ds(0, half), pl.ds(half, half)
            q0, q1 = qkv[lo, qc], qkv[hi, qc]
            k0, k1 = qkv[lo, kc], qkv[hi, kc]
            v0, v1 = qkv[lo, vc], qkv[hi, vc]
            s00 = lax.dot_general(q0, k0, nt, preferred_element_type=F32)
            s10 = lax.dot_general(q1, k0, nt, preferred_element_type=F32)
            s11 = lax.dot_general(q1, k1, nt, preferred_element_type=F32)
            s00 = jnp.where(tri, s00, 0.0).astype(BF16)
            s11 = jnp.where(tri, s11, 0.0).astype(BF16)
            s10 = s10.astype(BF16)
            yc = pl.ds(h * HD, HD)
            y[lo, yc] = jnp.dot(s00, v0, preferred_element_type=F32)
            y[hi, yc] = jnp.dot(s10, v0, preferred_element_type=F32) + jnp.dot(s11, v1, preferred_element_type=F32)

    def finish(qkv, y, pf, core, dst):
        for h in range(NH):
            cols = pl.ds(h * HD, HD)
            inter = jnp.dot(qkv[:, cols], pf[pl.ds(h * HD, HD), :], preferred_element_type=F32)
            total = y[:, cols] + inter
            scale = lax.rsqrt(jnp.mean(total * total, axis=-1, keepdims=True) + 1e-06)
            dst[:, cols] = (total * scale * gain_ref[pl.ds(core * NH + h, 1), :]).astype(BF16)

    loads[0].wait()
    loads[1].wait()
    project(x_own, 1, qkv_a)
    loads[2].wait()
    project(x_own, 2, qkv_a)
    state(qkv_a, kv_a)
    scatter_start(kv_a, r1a, f, 0, 1)
    r1a[p] = kv_a[rows(p), :]
    send_x.wait_recv()
    send_wo.start()

    project(x_oth, 1, qkv_s)
    project(x_oth, 2, qkv_s)
    state(qkv_s, kv_b)
    scatter_start(kv_b, r1b, g, 1, 0)
    send_k.start()
    scatter_wait(kv_a, r1a, 0, 1)
    totals_start(r1a, t2a, r2a, 0)
    loads[3].wait()
    project(x_oth, 0, qkv_s)
    send_q.start()
    scatter_wait(kv_b, r1b, 1, 0)
    totals_start(r1b, t2b, r2b, 1)
    prefix_start(r1a, t2a, r2a, o3a, pfa, 0)
    project(x_own, 0, qkv_a)
    prefix_start(r1b, t2b, r2b, o3b, pfb, 1)
    intra(qkv_a, y_a)
    send_k.wait_recv()
    send_q.wait_recv()
    intra(qkv_r, y_b)
    prefix_wait(pfa, 0)
    finish(qkv_a, y_a, pfa, f, n_a)
    loads[4].wait()

    @pl.loop(0, 4)
    def _(i):
        cols = pl.ds(pl.multiple_of(i * 512, 512), 512)
        acc[:, cols] = jnp.dot(n_a[...], wo_own[:, cols], preferred_element_type=F32)

    prefix_wait(pfb, 1)
    finish(qkv_r, y_b, pfb, g, n_b)
    send_wo.wait_recv()

    def out_copy(i):
        cols = pl.ds(pl.multiple_of(i * 512, 512), 512)
        return pltpu.make_async_copy(out_v.at[:, cols], out_hbm.at[0, :, cols], st_sem.at[i])

    @pl.loop(0, 4)
    def _(i):
        cols = pl.ds(pl.multiple_of(i * 512, 512), 512)
        mixed = acc[:, cols] + jnp.dot(n_b[...], wo_oth[:, cols], preferred_element_type=F32)
        out_v[:, cols] = mixed.astype(BF16)
        out_copy(i).start()

    for copy in (send_x, send_wo, send_k, send_q):
        copy.wait_send()
    for n, first in ((0, 1), (1, 0)):
        kv = (kv_a, kv_b)[n]
        span = pl.ds(0, (PLANE - first) * SL)
        remote(kv.at[span], kv.at[span], s1_sem.at[n], q1_sem.at[n], partner).wait_send()
        span = pl.ds(0, (PLANE - 1) * SL)
        remote(kv.at[span], kv.at[span], s3_sem.at[n], q3_sem.at[n], partner).wait_send()
        tot = (t2a, t2b)[n]
        for k in range(1, NZ):
            @pl.when(z + k < NZ)
            def _():
                remote(tot, tot, s2_sem.at[n, k], q2_sem.at[n, k], partner).wait_send()
    for i in range(4):
        out_copy(i).wait()


def body(tokens, w_qkv, w_out, gain):
    w = jnp.transpose(w_qkv, (1, 0, 2))
    any_ = pl.BlockSpec(memory_space=pl.ANY)
    vm = pltpu.VMEM
    dma = pltpu.SemaphoreType.DMA
    scratch = [
        vm((T, D), BF16), vm((T, D), BF16), vm((3, D, HC), BF16), vm((HC, D), BF16), vm((HC, D), BF16),
        vm((T, 3 * HC), BF16), vm((T, 3 * HC), BF16), vm((T, 3 * HC), BF16),
        vm((HC, HD), BF16), vm((HC, HD), BF16),
        vm((PLANE, SL, HD), BF16), vm((PLANE, SL, HD), BF16),
        vm((SL, HD), BF16), vm((SL, HD), BF16),
        vm((NZ, SL, HD), BF16), vm((NZ, SL, HD), BF16),
        vm((PLANE, SL, HD), BF16), vm((PLANE, SL, HD), BF16),
        vm((HC, HD), BF16), vm((HC, HD), BF16),
        vm((T, HC), F32), vm((T, HC), F32), vm((T, HC), BF16), vm((T, HC), BF16),
        vm((T, D), F32), vm((T, D), BF16),
        dma((5,)), dma((4,)), dma((4,)), dma((4,)),
        dma((2,)), dma((2,)), dma((2, NZ)), dma((2, NZ)), dma((2,)), dma((2,)),
    ]
    return pl.pallas_call(
        kernel,
        out_shape=jax.ShapeDtypeStruct((1, T, D), BF16),
        in_specs=[any_, any_, any_, pl.BlockSpec(memory_space=pltpu.VMEM)],
        out_specs=any_,
        scratch_shapes=scratch,
        compiler_params=pltpu.CompilerParams(
            collective_id=0, has_side_effects=True, vmem_limit_bytes=56 * 1024 * 1024
        ),
        cost_estimate=pl.CostEstimate(flops=10_000_000_000, bytes_accessed=14_000_000, transcendentals=1_600_000),
    )(tokens, w, w_out, gain.reshape(2 * NH, HD))


def solution(mesh):
    in_specs = (P("fsdp", "ctx", None), P(None, None, "fsdp"), P("fsdp", None), P())
    out_specs = P("fsdp", "ctx", None)
    return jax.shard_map(body, mesh=mesh, in_specs=in_specs, out_specs=out_specs, check_vma=False)
```

```python
import jax
import jax.numpy as jnp
from jax import lax
from jax.experimental import pallas as pl
from jax.experimental.pallas import tpu as pltpu
from jax.sharding import PartitionSpec as P

HD = 128
T = 512
D = 2048
NH = 4
HC = NH * HD
PLANE = 16
NZ = 8
SL = HC // PLANE
F32 = jnp.float32
BF16 = jnp.bfloat16
MESH = pl.DeviceIdType.MESH
FAR = sorted(((dx, dy) for dx in range(4) for dy in range(4)), key=lambda o: -min(o[0], 4 - o[0]) - min(o[1], 4 - o[1]))
FARZ = (4, 3, 5, 2, 6, 1, 7)


def silu(v):
    half = 0.5 * v
    return half + half * jnp.tanh(half)


def remote(src, dst, send, recv, device):
    return pltpu.make_async_remote_copy(
        src_ref=src, dst_ref=dst, send_sem=send, recv_sem=recv, device_id=device, device_id_type=MESH
    )


def kernel(
    x_hbm, w_hbm, wo_hbm, gain_hbm,
    acc, n_b, wo_oth,
    x_own, x_oth, w, wo_own, gain_ref,
    qkv_a, qkv_s, qkv_r,
    kv_a, kv_b, r1a, r1b, t2a, t2b, r2a, r2b, o3a, o3b, pfa, pfb,
    y_a, y_b, n_a,
    ld_sem, ps_sem, pr_sem, s1_sem, q1_sem, s2_sem, q2_sem, s3_sem, q3_sem,
):
    f = lax.axis_index("fsdp")
    c = lax.axis_index("ctx")
    z = c // PLANE
    p = lax.rem(c, PLANE)
    base = z * PLANE
    g = 1 - f

    px, py = p // 4, lax.rem(p, 4)

    def chip(k):
        dx, dy = FAR[k]
        return lax.rem(px + dx, 4) * 4 + lax.rem(py + dy, 4)

    def plane(k):
        return lax.rem(z + FARZ[k], NZ) * PLANE + p

    barrier = pltpu.get_barrier_semaphore()
    for k in range(PLANE):
        if k < NZ - 1:
            pl.semaphore_signal(barrier, inc=1, device_id=(f, plane(k)), device_id_type=MESH)
        pl.semaphore_signal(barrier, inc=1, device_id=(g, base + chip(k)), device_id_type=MESH)
        if k < PLANE - 1:
            pl.semaphore_signal(barrier, inc=1, device_id=(f, base + chip(k)), device_id_type=MESH)

    loads = [pltpu.make_async_copy(x_hbm.at[0], x_own, ld_sem.at[0])]
    for n, which in enumerate((1, 2, 0)):
        loads.append(pltpu.make_async_copy(w_hbm.at[which], w.at[which], ld_sem.at[1 + n]))
    loads.append(pltpu.make_async_copy(wo_hbm, wo_own, ld_sem.at[4]))
    loads.append(pltpu.make_async_copy(gain_hbm, gain_ref, ld_sem.at[5]))
    for copy in loads:
        copy.start()

    partner = (g, c)
    halves = [pl.ds(0, T // 2), pl.ds(T // 2, T // 2)]
    send_x = [
        remote(x_hbm.at[0, half], x_oth.at[half], ps_sem.at[4 + n], pr_sem.at[4 + n], partner)
        for n, half in enumerate(halves)
    ]
    send_wo = remote(wo_hbm, wo_oth, ps_sem.at[1], pr_sem.at[1], partner)
    send_k = remote(
        qkv_s.at[:, pl.ds(HC, 2 * HC)], qkv_r.at[:, pl.ds(HC, 2 * HC)], ps_sem.at[2], pr_sem.at[2], partner
    )
    send_q = remote(qkv_s.at[:, pl.ds(0, HC)], qkv_r.at[:, pl.ds(0, HC)], ps_sem.at[3], pr_sem.at[3], partner)

    def project(x, which, dst, rows=pl.ds(0, T)):
        part = jnp.dot(x[rows, :], w[which], preferred_element_type=F32)
        dst[rows, pl.ds(which * HC, HC)] = silu(part).astype(BF16)

    def state(qkv, dst):
        for h in range(NH):
            key = qkv[:, pl.ds(HC + h * HD, HD)]
            val = qkv[:, pl.ds(2 * HC + h * HD, HD)]
            kv = lax.dot_general(key, val, (((0,), (0,)), ((), ())), preferred_element_type=F32)
            dst[pl.ds(h * HD, HD), :] = kv.astype(BF16)

    def rows(i):
        return pl.ds(pl.multiple_of(i * SL, SL), SL)

    def scatter_start(kv, got, core, n, first):
        for k in range(PLANE - first):
            j = chip(k)
            remote(kv.at[rows(j)], got.at[p], s1_sem.at[n], q1_sem.at[n], (core, base + j)).start()

    def scatter_wait(kv, got, n, first):
        m = PLANE - first
        remote(kv.at[pl.ds(0, m * SL)], kv.at[pl.ds(0, m * SL)], s1_sem.at[n], q1_sem.at[n], partner).wait_recv()

    def totals_start(got, tot, r2, n):
        total = got[0].astype(F32)
        for i in range(1, PLANE):
            total = total + got[i].astype(F32)
        tot[...] = total.astype(BF16)
        for k in (4, 3, 5, 2, 6, 1, 7):
            @pl.when(z + k < NZ)
            def _():
                remote(
                    tot, r2.at[z], s2_sem.at[n, k], q2_sem.at[n, z], (f, (z + k) * PLANE + p)
                ).start()

    def prefix_start(got, tot, r2, o3, pf, n):
        def add(i, total):
            remote(tot, r2.at[i], s2_sem.at[n, 0], q2_sem.at[n, i], partner).wait_recv()
            return total + r2[i].astype(F32)

        total = lax.fori_loop(0, z, add, jnp.zeros((SL, HD), F32))
        for i in range(PLANE):
            o3[i] = total.astype(BF16)
            if i < PLANE - 1:
                total = total + got[i].astype(F32)
        for k in range(PLANE - 1):
            j = chip(k)
            remote(o3.at[j], pf.at[rows(p)], s3_sem.at[n], q3_sem.at[n], (f, base + j)).start()
        pf[rows(p), :] = o3[p]

    def prefix_wait(pf, n):
        m = PLANE - 1
        remote(pf.at[pl.ds(0, m * SL)], pf.at[pl.ds(0, m * SL)], s3_sem.at[n], q3_sem.at[n], partner).wait_recv()

    half = T // 2
    tri = lax.broadcasted_iota(jnp.int32, (half, half), 0) >= lax.broadcasted_iota(jnp.int32, (half, half), 1)

    def intra(qkv, y):
        nt = (((1,), (1,)), ((), ()))
        for h in range(NH):
            qc, kc, vc = (pl.ds(n * HC + h * HD, HD) for n in range(3))
            lo, hi = pl.ds(0, half), pl.ds(half, half)
            q0, q1 = qkv[lo, qc], qkv[hi, qc]
            k0, k1 = qkv[lo, kc], qkv[hi, kc]
            v0, v1 = qkv[lo, vc], qkv[hi, vc]
            s00 = lax.dot_general(q0, k0, nt, preferred_element_type=F32)
            s10 = lax.dot_general(q1, k0, nt, preferred_element_type=F32)
            s11 = lax.dot_general(q1, k1, nt, preferred_element_type=F32)
            s00 = jnp.where(tri, s00, 0.0).astype(BF16)
            s11 = jnp.where(tri, s11, 0.0).astype(BF16)
            s10 = s10.astype(BF16)
            yc = pl.ds(h * HD, HD)
            y[lo, yc] = jnp.dot(s00, v0, preferred_element_type=F32)
            y[hi, yc] = jnp.dot(s10, v0, preferred_element_type=F32) + jnp.dot(s11, v1, preferred_element_type=F32)

    def finish(qkv, y, pf, core, dst):
        for h in range(NH):
            cols = pl.ds(h * HD, HD)
            inter = jnp.dot(qkv[:, cols], pf[pl.ds(h * HD, HD), :], preferred_element_type=F32)
            total = y[:, cols] + inter
            scale = lax.rsqrt(jnp.mean(total * total, axis=-1, keepdims=True) + 1e-06)
            dst[:, cols] = (total * scale * gain_ref[pl.ds(core * NH + h, 1), :]).astype(BF16)

    loads[0].wait()
    loads[1].wait()
    project(x_own, 1, qkv_a)
    pl.semaphore_wait(barrier, 2 * PLANE - 1 + NZ - 1)
    for copy in send_x:
        copy.start()
    loads[2].wait()
    project(x_own, 2, qkv_a)
    state(qkv_a, kv_a)
    scatter_start(kv_a, r1a, f, 0, 1)
    r1a[p] = kv_a[rows(p), :]
    loads[3].wait()
    project(x_own, 0, qkv_a)

    for copy, half_rows in zip(send_x, halves):
        copy.wait_recv()
        project(x_oth, 1, qkv_s, half_rows)
        project(x_oth, 2, qkv_s, half_rows)
    state(qkv_s, kv_b)
    scatter_start(kv_b, r1b, g, 1, 0)
    send_k.start()
    project(x_oth, 0, qkv_s)
    send_q.start()
    send_wo.start()
    scatter_wait(kv_a, r1a, 0, 1)
    totals_start(r1a, t2a, r2a, 0)
    intra(qkv_a, y_a)
    scatter_wait(kv_b, r1b, 1, 0)
    totals_start(r1b, t2b, r2b, 1)
    prefix_start(r1a, t2a, r2a, o3a, pfa, 0)
    send_k.wait_recv()
    send_q.wait_recv()
    intra(qkv_r, y_b)
    prefix_start(r1b, t2b, r2b, o3b, pfb, 1)
    prefix_wait(pfa, 0)
    loads[5].wait()
    finish(qkv_a, y_a, pfa, f, n_a)
    loads[4].wait()

    @pl.loop(0, 4)
    def _(i):
        cols = pl.ds(pl.multiple_of(i * 512, 512), 512)
        acc[:, cols] = jnp.dot(n_a[...], wo_own[:, cols], preferred_element_type=F32)

    send_wo.wait_recv()
    for copy in (*send_x, send_wo, send_k, send_q):
        copy.wait_send()
    for n, first in ((0, 1), (1, 0)):
        kv = (kv_a, kv_b)[n]
        span = pl.ds(0, (PLANE - first) * SL)
        remote(kv.at[span], kv.at[span], s1_sem.at[n], q1_sem.at[n], partner).wait_send()
        tot = (t2a, t2b)[n]
        for k in range(1, NZ):
            @pl.when(z + k < NZ)
            def _():
                remote(tot, tot, s2_sem.at[n, k], q2_sem.at[n, k], partner).wait_send()

    prefix_wait(pfb, 1)
    finish(qkv_r, y_b, pfb, g, n_b)
    span = pl.ds(0, (PLANE - 1) * SL)
    for n in range(2):
        remote(kv_a.at[span], kv_a.at[span], s3_sem.at[n], q3_sem.at[n], partner).wait_send()


def out_kernel(acc, n_b, wo_oth, out):
    cols = pl.ds(pl.multiple_of(pl.program_id(0) * 512, 512), 512)
    mixed = acc[:, cols] + jnp.dot(n_b[...], wo_oth[:, cols], preferred_element_type=F32)
    out[0] = mixed.astype(BF16)


def body(tokens, w_qkv, w_out, gain):
    w = jnp.transpose(w_qkv, (1, 0, 2))
    any_ = pl.BlockSpec(memory_space=pl.ANY)
    vm = pltpu.VMEM
    dma = pltpu.SemaphoreType.DMA
    scratch = [
        vm((T, D), BF16), vm((T, D), BF16), vm((3, D, HC), BF16), vm((HC, D), BF16), vm((2 * NH, HD), F32),
        vm((T, 3 * HC), BF16), vm((T, 3 * HC), BF16), vm((T, 3 * HC), BF16),
        vm((HC, HD), BF16), vm((HC, HD), BF16),
        vm((PLANE, SL, HD), BF16), vm((PLANE, SL, HD), BF16),
        vm((SL, HD), BF16), vm((SL, HD), BF16),
        vm((NZ, SL, HD), BF16), vm((NZ, SL, HD), BF16),
        vm((PLANE, SL, HD), BF16), vm((PLANE, SL, HD), BF16),
        vm((HC, HD), BF16), vm((HC, HD), BF16),
        vm((T, HC), F32), vm((T, HC), F32), vm((T, HC), BF16),
        dma((6,)), dma((6,)), dma((6,)),
        dma((2,)), dma((2,)), dma((2, NZ)), dma((2, NZ)), dma((2,)), dma((2,)),
    ]
    whole = pl.BlockSpec(memory_space=pltpu.VMEM)
    acc, n_b, wo_oth = pl.pallas_call(
        kernel,
        out_shape=[pltpu.VMEM((T, D), F32), pltpu.VMEM((T, HC), BF16), pltpu.VMEM((HC, D), BF16)],
        in_specs=[any_] * 4,
        out_specs=[whole, whole, whole],
        scratch_shapes=scratch,
        compiler_params=pltpu.CompilerParams(
            collective_id=0, has_side_effects=True, vmem_limit_bytes=32 * 1024 * 1024
        ),
        cost_estimate=pl.CostEstimate(flops=9_000_000_000, bytes_accessed=12_000_000, transcendentals=1_600_000),
    )(*(pltpu.with_memory_space_constraint(a, pltpu.HBM) for a in (tokens, w, w_out, gain.reshape(2 * NH, HD))))
    return pl.pallas_call(
        out_kernel,
        out_shape=jax.ShapeDtypeStruct((1, T, D), BF16),
        grid=(4,),
        in_specs=[whole, whole, whole],
        out_specs=pl.BlockSpec((1, T, 512), lambda i: (0, 0, i)),
        compiler_params=pltpu.CompilerParams(vmem_limit_bytes=16 * 1024 * 1024),
        cost_estimate=pl.CostEstimate(flops=1_000_000_000, bytes_accessed=2_000_000, transcendentals=0),
    )(acc, n_b, wo_oth)


def solution(mesh):
    in_specs = (P("fsdp", "ctx", None), P(None, None, "fsdp"), P("fsdp", None), P())
    out_specs = P("fsdp", "ctx", None)
    return jax.shard_map(body, mesh=mesh, in_specs=in_specs, out_specs=out_specs, check_vma=False)
```

```python
import jax
import jax.numpy as jnp
from jax import lax
from jax.experimental import pallas as pl
from jax.experimental.pallas import tpu as pltpu
from jax.sharding import PartitionSpec as P

HD = 128
T = 512
D = 2048
NH = 4
HC = NH * HD
PLANE = 16
NZ = 8
SL = HC // PLANE
F32 = jnp.float32
BF16 = jnp.bfloat16
MESH = pl.DeviceIdType.MESH
FAR = sorted(((dx, dy) for dx in range(4) for dy in range(4)), key=lambda o: -min(o[0], 4 - o[0]) - min(o[1], 4 - o[1]))


def silu(v):
    half = 0.5 * v
    return half + half * jnp.tanh(half)


def remote(src, dst, send, recv, device):
    return pltpu.make_async_remote_copy(
        src_ref=src, dst_ref=dst, send_sem=send, recv_sem=recv, device_id=device, device_id_type=MESH
    )


def kernel(
    x_hbm, w_hbm, wo_hbm, gain_hbm,
    acc, n_b, wo_oth,
    x_own, x_oth, w, wo_own, gain_ref,
    qkv_a, qkv_s, qkv_r,
    kv_a, kv_b, r1a, r1b, t2a, t2b, r2a, r2b, o3a, o3b, pfa, pfb,
    y_a, y_b, n_a,
    ld_sem, ps_sem, pr_sem, s1_sem, q1_sem, s2_sem, q2_sem, s3_sem, q3_sem, in_sem,
):
    f = lax.axis_index("fsdp")
    c = lax.axis_index("ctx")
    z = c // PLANE
    p = lax.rem(c, PLANE)
    base = z * PLANE
    g = 1 - f

    px, py = p // 4, lax.rem(p, 4)

    def chip(k):
        dx, dy = FAR[k]
        return lax.rem(px + dx, 4) * 4 + lax.rem(py + dy, 4)

    def tell(sem, core, plane, spot):
        pl.semaphore_signal(sem, inc=1, device_id=(core, plane * PLANE + spot), device_id_type=MESH)

    def at(dx, dy):
        return lax.rem(px + dx, 4) * 4 + lax.rem(py + dy, 4)

    near = ((1, 0), (3, 0), (0, 1), (0, 3))
    barrier = pltpu.get_barrier_semaphore()
    tell(barrier, g, z, p)
    for dx, dy in near:
        tell(barrier, f, z, at(dx, dy))
    for k in (4, 3, 5, 2, 6, 1, 7):
        @pl.when(z + k < NZ)
        def _():
            tell(barrier, f, z + k, p)

    loads = [pltpu.make_async_copy(x_hbm.at[0], x_own, ld_sem.at[0])]
    for n, which in enumerate((1, 2, 0)):
        loads.append(pltpu.make_async_copy(w_hbm.at[which], w.at[which], ld_sem.at[1 + n]))
    loads.append(pltpu.make_async_copy(wo_hbm, wo_own, ld_sem.at[4]))
    loads.append(pltpu.make_async_copy(gain_hbm, gain_ref, ld_sem.at[5]))
    for copy in loads:
        copy.start()

    partner = (g, c)
    halves = [pl.ds(0, T // 2), pl.ds(T // 2, T // 2)]
    send_x = [
        remote(x_hbm.at[0, half], x_oth.at[half], ps_sem.at[4 + n], pr_sem.at[4 + n], partner)
        for n, half in enumerate(halves)
    ]
    send_wo = remote(wo_hbm, wo_oth, ps_sem.at[1], pr_sem.at[1], partner)
    send_k = remote(
        qkv_s.at[:, pl.ds(HC, 2 * HC)], qkv_r.at[:, pl.ds(HC, 2 * HC)], ps_sem.at[2], pr_sem.at[2], partner
    )
    send_q = remote(qkv_s.at[:, pl.ds(0, HC)], qkv_r.at[:, pl.ds(0, HC)], ps_sem.at[3], pr_sem.at[3], partner)

    def project(x, which, dst, rows=pl.ds(0, T)):
        part = jnp.dot(x[rows, :], w[which], preferred_element_type=F32)
        dst[rows, pl.ds(which * HC, HC)] = silu(part).astype(BF16)

    def state(qkv, dst):
        for h in range(NH):
            key = qkv[:, pl.ds(HC + h * HD, HD)]
            val = qkv[:, pl.ds(2 * HC + h * HD, HD)]
            kv = lax.dot_general(key, val, (((0,), (0,)), ((), ())), preferred_element_type=F32)
            dst[pl.ds(h * HD, HD), :] = kv.astype(BF16)

    def rows(i):
        return pl.ds(pl.multiple_of(i * SL, SL), SL)

    def scatter_start(kv, got, core, n, first):
        for k in range(PLANE - first):
            j = chip(k)
            remote(kv.at[rows(j)], got.at[p], s1_sem.at[n], q1_sem.at[n], (core, base + j)).start()

    def scatter_wait(kv, got, n, first):
        m = PLANE - first
        remote(kv.at[pl.ds(0, m * SL)], kv.at[pl.ds(0, m * SL)], s1_sem.at[n], q1_sem.at[n], partner).wait_recv()

    def totals_start(got, tot, r2, n):
        total = got[0].astype(F32)
        for i in range(1, PLANE):
            total = total + got[i].astype(F32)
        tot[...] = total.astype(BF16)
        for k in (4, 3, 5, 2, 6, 1, 7):
            @pl.when(z + k < NZ)
            def _():
                remote(
                    tot, r2.at[z], s2_sem.at[n, k], q2_sem.at[n, z], (f, (z + k) * PLANE + p)
                ).start()

    def prefix_start(got, tot, r2, o3, pf, n):
        def add(i, total):
            remote(tot, r2.at[i], s2_sem.at[n, 0], q2_sem.at[n, i], partner).wait_recv()
            return total + r2[i].astype(F32)

        total = lax.fori_loop(0, z, add, jnp.zeros((SL, HD), F32))
        for i in range(PLANE):
            o3[i] = total.astype(BF16)
            if i < PLANE - 1:
                total = total + got[i].astype(F32)
        for k in range(PLANE - 1):
            j = chip(k)
            remote(o3.at[j], pf.at[rows(p)], s3_sem.at[n], q3_sem.at[n], (f, base + j)).start()
        pf[rows(p), :] = o3[p]

    def prefix_wait(pf, n):
        m = PLANE - 1
        remote(pf.at[pl.ds(0, m * SL)], pf.at[pl.ds(0, m * SL)], s3_sem.at[n], q3_sem.at[n], partner).wait_recv()

    half = T // 2
    tri = lax.broadcasted_iota(jnp.int32, (half, half), 0) >= lax.broadcasted_iota(jnp.int32, (half, half), 1)

    def intra(qkv, y):
        nt = (((1,), (1,)), ((), ()))
        for h in range(NH):
            qc, kc, vc = (pl.ds(n * HC + h * HD, HD) for n in range(3))
            lo, hi = pl.ds(0, half), pl.ds(half, half)
            q0, q1 = qkv[lo, qc], qkv[hi, qc]
            k0, k1 = qkv[lo, kc], qkv[hi, kc]
            v0, v1 = qkv[lo, vc], qkv[hi, vc]
            s00 = lax.dot_general(q0, k0, nt, preferred_element_type=F32)
            s10 = lax.dot_general(q1, k0, nt, preferred_element_type=F32)
            s11 = lax.dot_general(q1, k1, nt, preferred_element_type=F32)
            s00 = jnp.where(tri, s00, 0.0).astype(BF16)
            s11 = jnp.where(tri, s11, 0.0).astype(BF16)
            s10 = s10.astype(BF16)
            yc = pl.ds(h * HD, HD)
            y[lo, yc] = jnp.dot(s00, v0, preferred_element_type=F32)
            y[hi, yc] = jnp.dot(s10, v0, preferred_element_type=F32) + jnp.dot(s11, v1, preferred_element_type=F32)

    def finish(qkv, y, pf, core, dst):
        for h in range(NH):
            cols = pl.ds(h * HD, HD)
            inter = jnp.dot(qkv[:, cols], pf[pl.ds(h * HD, HD), :], preferred_element_type=F32)
            total = y[:, cols] + inter
            scale = lax.rsqrt(jnp.mean(total * total, axis=-1, keepdims=True) + 1e-06)
            dst[:, cols] = (total * scale * gain_ref[pl.ds(core * NH + h, 1), :]).astype(BF16)

    pl.semaphore_wait(barrier, 5 + z)
    for copy in send_x:
        copy.start()
    tell(in_sem.at[0], g, z, p)
    for dx, dy in near:
        tell(in_sem.at[0], f, z, at(dx, dy))
    for k in (4, 3, 5, 2, 6, 1, 7):
        @pl.when(z - k >= 0)
        def _():
            tell(in_sem.at[3], f, z - k, p)

    loads[0].wait()
    loads[1].wait()
    project(x_own, 1, qkv_a)
    pl.semaphore_wait(in_sem.at[0], 5)
    tell(in_sem.at[1], f, z, at(2, 0))
    tell(in_sem.at[1], f, z, at(0, 2))
    tell(in_sem.at[1], g, z, p)
    loads[2].wait()
    project(x_own, 2, qkv_a)
    state(qkv_a, kv_a)
    pl.semaphore_wait(in_sem.at[1], 3)
    tell(in_sem.at[2], g, z, p)
    scatter_start(kv_a, r1a, f, 0, 1)
    r1a[p] = kv_a[rows(p), :]

    for copy, half_rows in zip(send_x, halves):
        copy.wait_recv()
        project(x_oth, 1, qkv_s, half_rows)
        project(x_oth, 2, qkv_s, half_rows)
    state(qkv_s, kv_b)
    pl.semaphore_wait(in_sem.at[2], 1)
    scatter_start(kv_b, r1b, g, 1, 0)
    send_k.start()
    loads[3].wait()
    project(x_oth, 0, qkv_s)
    send_q.start()
    send_wo.start()
    project(x_own, 0, qkv_a)
    scatter_wait(kv_a, r1a, 0, 1)

    @pl.when(z < NZ - 1)
    def _():
        pl.semaphore_wait(in_sem.at[3], NZ - 1 - z)

    totals_start(r1a, t2a, r2a, 0)
    intra(qkv_a, y_a)
    scatter_wait(kv_b, r1b, 1, 0)
    totals_start(r1b, t2b, r2b, 1)
    prefix_start(r1a, t2a, r2a, o3a, pfa, 0)
    prefix_start(r1b, t2b, r2b, o3b, pfb, 1)
    send_k.wait_recv()
    send_q.wait_recv()
    intra(qkv_r, y_b)
    prefix_wait(pfa, 0)
    loads[5].wait()
    finish(qkv_a, y_a, pfa, f, n_a)
    loads[4].wait()

    @pl.loop(0, 4)
    def _(i):
        cols = pl.ds(pl.multiple_of(i * 512, 512), 512)
        acc[:, cols] = jnp.dot(n_a[...], wo_own[:, cols], preferred_element_type=F32)

    send_wo.wait_recv()
    for copy in (*send_x, send_wo, send_k, send_q):
        copy.wait_send()
    for n, first in ((0, 1), (1, 0)):
        kv = (kv_a, kv_b)[n]
        span = pl.ds(0, (PLANE - first) * SL)
        remote(kv.at[span], kv.at[span], s1_sem.at[n], q1_sem.at[n], partner).wait_send()
        tot = (t2a, t2b)[n]
        for k in range(1, NZ):
            @pl.when(z + k < NZ)
            def _():
                remote(tot, tot, s2_sem.at[n, k], q2_sem.at[n, k], partner).wait_send()

    prefix_wait(pfb, 1)
    finish(qkv_r, y_b, pfb, g, n_b)
    span = pl.ds(0, (PLANE - 1) * SL)
    for n in range(2):
        remote(kv_a.at[span], kv_a.at[span], s3_sem.at[n], q3_sem.at[n], partner).wait_send()


def out_kernel(acc, n_b, wo_oth, out):
    cols = pl.ds(pl.multiple_of(pl.program_id(0) * 512, 512), 512)
    mixed = acc[:, cols] + jnp.dot(n_b[...], wo_oth[:, cols], preferred_element_type=F32)
    out[0] = mixed.astype(BF16)


def body(tokens, w_qkv, w_out, gain):
    w = jnp.transpose(w_qkv, (1, 0, 2))
    any_ = pl.BlockSpec(memory_space=pl.ANY)
    vm = pltpu.VMEM
    dma = pltpu.SemaphoreType.DMA
    scratch = [
        vm((T, D), BF16), vm((T, D), BF16), vm((3, D, HC), BF16), vm((HC, D), BF16), vm((2 * NH, HD), F32),
        vm((T, 3 * HC), BF16), vm((T, 3 * HC), BF16), vm((T, 3 * HC), BF16),
        vm((HC, HD), BF16), vm((HC, HD), BF16),
        vm((PLANE, SL, HD), BF16), vm((PLANE, SL, HD), BF16),
        vm((SL, HD), BF16), vm((SL, HD), BF16),
        vm((NZ, SL, HD), BF16), vm((NZ, SL, HD), BF16),
        vm((PLANE, SL, HD), BF16), vm((PLANE, SL, HD), BF16),
        vm((HC, HD), BF16), vm((HC, HD), BF16),
        vm((T, HC), F32), vm((T, HC), F32), vm((T, HC), BF16),
        dma((6,)), dma((6,)), dma((6,)),
        dma((2,)), dma((2,)), dma((2, NZ)), dma((2, NZ)), dma((2,)), dma((2,)),
        pltpu.SemaphoreType.REGULAR((4,)),
    ]
    whole = pl.BlockSpec(memory_space=pltpu.VMEM)
    acc, n_b, wo_oth = pl.pallas_call(
        kernel,
        out_shape=[pltpu.VMEM((T, D), F32), pltpu.VMEM((T, HC), BF16), pltpu.VMEM((HC, D), BF16)],
        in_specs=[any_] * 4,
        out_specs=[whole, whole, whole],
        scratch_shapes=scratch,
        compiler_params=pltpu.CompilerParams(
            collective_id=0, has_side_effects=True, vmem_limit_bytes=32 * 1024 * 1024
        ),
        cost_estimate=pl.CostEstimate(flops=9_000_000_000, bytes_accessed=12_000_000, transcendentals=1_600_000),
    )(*(pltpu.with_memory_space_constraint(a, pltpu.HBM) for a in (tokens, w, w_out, gain.reshape(2 * NH, HD))))
    return pl.pallas_call(
        out_kernel,
        out_shape=jax.ShapeDtypeStruct((1, T, D), BF16),
        grid=(4,),
        in_specs=[whole, whole, whole],
        out_specs=pl.BlockSpec((1, T, 512), lambda i: (0, 0, i)),
        compiler_params=pltpu.CompilerParams(vmem_limit_bytes=16 * 1024 * 1024),
        cost_estimate=pl.CostEstimate(flops=1_000_000_000, bytes_accessed=2_000_000, transcendentals=0),
    )(acc, n_b, wo_oth)


def solution(mesh):
    in_specs = (P("fsdp", "ctx", None), P(None, None, "fsdp"), P("fsdp", None), P())
    out_specs = P("fsdp", "ctx", None)
    return jax.shard_map(body, mesh=mesh, in_specs=in_specs, out_specs=out_specs, check_vma=False)
```

```python
import jax
import jax.numpy as jnp
from jax import lax
from jax.experimental import pallas as pl
from jax.experimental.pallas import tpu as pltpu
from jax.sharding import PartitionSpec as P

HD = 128
T = 512
D = 2048
NH = 4
HC = NH * HD
PLANE = 16
NZ = 8
SL = HC // PLANE
F32 = jnp.float32
BF16 = jnp.bfloat16
MESH = pl.DeviceIdType.MESH
WIDTHS = (512, 512, 512, 256, 256)
FAR = sorted(((dx, dy) for dx in range(4) for dy in range(4)), key=lambda o: -min(o[0], 4 - o[0]) - min(o[1], 4 - o[1]))


def silu(v):
    half = 0.5 * v
    return half + half * jnp.tanh(half)


def remote(src, dst, send, recv, device):
    return pltpu.make_async_remote_copy(
        src_ref=src, dst_ref=dst, send_sem=send, recv_sem=recv, device_id=device, device_id_type=MESH
    )


def finish(qkv, y, pf, gain, row, dst):
    for h in range(NH):
        cols = pl.ds(h * HD, HD)
        inter = jnp.dot(qkv[:, cols], pf[cols, :], preferred_element_type=F32)
        total = y[:, cols] + inter
        scale = lax.rsqrt(jnp.mean(total * total, axis=-1, keepdims=True) + 1e-06)
        dst[:, cols] = (total * scale * gain[pl.ds(row + h, 1), :]).astype(BF16)


def kernel(
    x_hbm, w_hbm, wo_hbm, gain_hbm,
    acc, y_b, qkv_r, pfb, gain_b, wo_oth,
    x_own, x_oth, w, wo_own, gain_ref,
    qkv_a, qkv_s,
    kv_a, kv_b, r1a, r1b, t2a, t2b, r2a, r2b, o3a, o3b, pfa, kv_sum,
    y_a, n_a,
    ld_sem, ps_sem, pr_sem, s1_sem, q1_sem, s2_sem, q2_sem, s3_sem, q3_sem, in_sem,
):
    f = lax.axis_index("fsdp")
    c = lax.axis_index("ctx")
    z = c // PLANE
    p = lax.rem(c, PLANE)
    base = z * PLANE
    g = 1 - f

    px, py = p // 4, lax.rem(p, 4)

    def chip(k):
        dx, dy = FAR[k]
        return lax.rem(px + dx, 4) * 4 + lax.rem(py + dy, 4)

    def tell(sem, core, plane, spot):
        pl.semaphore_signal(sem, inc=1, device_id=(core, plane * PLANE + spot), device_id_type=MESH)

    def at(dx, dy):
        return lax.rem(px + dx, 4) * 4 + lax.rem(py + dy, 4)

    halves = [pl.ds(0, T // 2), pl.ds(T // 2, T // 2)]
    sources = (
        (x_hbm.at[0, halves[0]], x_own.at[halves[0]]), (w_hbm.at[1], w.at[1]),
        (x_hbm.at[0, halves[1]], x_own.at[halves[1]]), (w_hbm.at[2], w.at[2]),
        (w_hbm.at[0], w.at[0]), (wo_hbm, wo_own), (gain_hbm, gain_ref),
    )
    loads = [pltpu.make_async_copy(src, dst, ld_sem.at[n]) for n, (src, dst) in enumerate(sources)]
    for copy in loads[:4]:
        copy.start()

    near = ((1, 0), (3, 0), (0, 1), (0, 3))
    barrier = pltpu.get_barrier_semaphore()
    tell(barrier, g, z, p)
    for dx, dy in near:
        tell(barrier, f, z, at(dx, dy))
    for k in (4, 3, 5, 2, 6, 1, 7):
        @pl.when(z + k < NZ)
        def _():
            tell(barrier, f, z + k, p)

    partner = (g, c)
    parts = [pl.ds(0, T // 2), pl.ds(T // 2, T // 4), pl.ds(3 * T // 4, T // 4)]
    send_x = [
        remote(x_hbm.at[0, half], x_oth.at[half], ps_sem.at[4 + n], pr_sem.at[4 + n], partner)
        for n, half in enumerate(parts)
    ]
    send_wo = remote(wo_hbm, wo_oth, ps_sem.at[1], pr_sem.at[1], partner)
    send_k = remote(
        qkv_s.at[:, pl.ds(HC, 2 * HC)], qkv_r.at[:, pl.ds(HC, 2 * HC)], ps_sem.at[2], pr_sem.at[2], partner
    )
    send_q = remote(qkv_s.at[:, pl.ds(0, HC)], qkv_r.at[:, pl.ds(0, HC)], ps_sem.at[3], pr_sem.at[3], partner)

    def project(x, which, dst, rows=pl.ds(0, T)):
        part = jnp.dot(x[rows, :], w[which], preferred_element_type=F32)
        dst[rows, pl.ds(which * HC, HC)] = silu(part).astype(BF16)

    def state(qkv, dst, part=pl.ds(0, T), first=True, last=True):
        for h in range(NH):
            key = qkv[part, pl.ds(HC + h * HD, HD)]
            val = qkv[part, pl.ds(2 * HC + h * HD, HD)]
            kv = lax.dot_general(key, val, (((0,), (0,)), ((), ())), preferred_element_type=F32)
            head = pl.ds(h * HD, HD)
            if not first:
                kv = kv + kv_sum[head, :]
            if last:
                dst[head, :] = kv.astype(BF16)
            else:
                kv_sum[head, :] = kv

    def rows(i):
        return pl.ds(pl.multiple_of(i * SL, SL), SL)

    def scatter_start(kv, got, core, n, first):
        for k in range(PLANE - first):
            j = chip(k)
            remote(kv.at[rows(j)], got.at[p], s1_sem.at[n], q1_sem.at[n], (core, base + j)).start()

    def scatter_wait(kv, got, n, first):
        m = PLANE - first
        remote(kv.at[pl.ds(0, m * SL)], kv.at[pl.ds(0, m * SL)], s1_sem.at[n], q1_sem.at[n], partner).wait_recv()

    def totals_start(got, tot, r2, n):
        total = got[0].astype(F32)
        for i in range(1, PLANE):
            total = total + got[i].astype(F32)
        tot[...] = total.astype(BF16)
        for k in (4, 3, 5, 2, 6, 1, 7):
            @pl.when(z + k < NZ)
            def _():
                remote(
                    tot, r2.at[z], s2_sem.at[n, k], q2_sem.at[n, z], (f, (z + k) * PLANE + p)
                ).start()

    def prefix_start(got, tot, r2, o3, pf, n):
        def add(i, total):
            remote(tot, r2.at[i], s2_sem.at[n, 0], q2_sem.at[n, i], partner).wait_recv()
            return total + r2[i].astype(F32)

        total = lax.fori_loop(0, z, add, jnp.zeros((SL, HD), F32))
        for i in range(PLANE):
            o3[i] = total.astype(BF16)
            if i < PLANE - 1:
                total = total + got[i].astype(F32)
        for k in range(PLANE - 1):
            j = chip(k)
            remote(o3.at[j], pf.at[rows(p)], s3_sem.at[n], q3_sem.at[n], (f, base + j)).start()
        pf[rows(p), :] = o3[p]

    def prefix_wait(pf, n):
        m = PLANE - 1
        remote(pf.at[pl.ds(0, m * SL)], pf.at[pl.ds(0, m * SL)], s3_sem.at[n], q3_sem.at[n], partner).wait_recv()

    half = T // 2
    tri = lax.broadcasted_iota(jnp.int32, (half, half), 0) >= lax.broadcasted_iota(jnp.int32, (half, half), 1)

    def intra(qkv, y):
        nt = (((1,), (1,)), ((), ()))
        for h in range(NH):
            qc, kc, vc = (pl.ds(n * HC + h * HD, HD) for n in range(3))
            lo, hi = pl.ds(0, half), pl.ds(half, half)
            q0, q1 = qkv[lo, qc], qkv[hi, qc]
            k0, k1 = qkv[lo, kc], qkv[hi, kc]
            v0, v1 = qkv[lo, vc], qkv[hi, vc]
            s00 = lax.dot_general(q0, k0, nt, preferred_element_type=F32)
            s10 = lax.dot_general(q1, k0, nt, preferred_element_type=F32)
            s11 = lax.dot_general(q1, k1, nt, preferred_element_type=F32)
            s00 = jnp.where(tri, s00, 0.0).astype(BF16)
            s11 = jnp.where(tri, s11, 0.0).astype(BF16)
            s10 = s10.astype(BF16)
            yc = pl.ds(h * HD, HD)
            y[lo, yc] = jnp.dot(s00, v0, preferred_element_type=F32)
            y[hi, yc] = jnp.dot(s10, v0, preferred_element_type=F32) + jnp.dot(s11, v1, preferred_element_type=F32)

    pl.semaphore_wait(barrier, 5 + z)
    for copy in (*send_x, *loads[4:]):
        copy.start()
    tell(in_sem.at[0], g, z, p)
    for dx, dy in near:
        tell(in_sem.at[0], f, z, at(dx, dy))
    for k in (4, 3, 5, 2, 6, 1, 7):
        @pl.when(z - k >= 0)
        def _():
            tell(in_sem.at[3], f, z - k, p)

    for n in range(2):
        loads[n].wait()
        if n:
            project(x_own, 1, qkv_a, halves[0])
    loads[2].wait()
    project(x_own, 1, qkv_a, halves[1])
    pl.semaphore_wait(in_sem.at[0], 5)
    tell(in_sem.at[1], f, z, at(2, 0))
    tell(in_sem.at[1], f, z, at(0, 2))
    tell(in_sem.at[1], g, z, p)
    loads[3].wait()
    project(x_own, 2, qkv_a)
    state(qkv_a, kv_a)
    pl.semaphore_wait(in_sem.at[1], 3)
    tell(in_sem.at[2], g, z, p)
    scatter_start(kv_a, r1a, f, 0, 1)
    r1a[p] = kv_a[rows(p), :]

    for n, (copy, part) in enumerate(zip(send_x, parts)):
        copy.wait_recv()
        project(x_oth, 1, qkv_s, part)
        project(x_oth, 2, qkv_s, part)
        state(qkv_s, kv_b, part, n == 0, n == 2)
    pl.semaphore_wait(in_sem.at[2], 1)
    scatter_start(kv_b, r1b, g, 1, 0)
    send_k.start()
    loads[4].wait()
    project(x_oth, 0, qkv_s)
    send_q.start()
    send_wo.start()
    project(x_own, 0, qkv_a)
    scatter_wait(kv_a, r1a, 0, 1)

    @pl.when(z < NZ - 1)
    def _():
        pl.semaphore_wait(in_sem.at[3], NZ - 1 - z)

    totals_start(r1a, t2a, r2a, 0)
    intra(qkv_a, y_a)
    scatter_wait(kv_b, r1b, 1, 0)
    totals_start(r1b, t2b, r2b, 1)
    prefix_start(r1a, t2a, r2a, o3a, pfa, 0)
    prefix_start(r1b, t2b, r2b, o3b, pfb, 1)
    send_k.wait_recv()
    send_q.wait_recv()
    intra(qkv_r, y_b)
    prefix_wait(pfa, 0)
    loads[6].wait()
    finish(qkv_a, y_a, pfa, gain_ref, f * NH, n_a)
    loads[5].wait()

    for i in range(4):
        cols = pl.ds(i * 512, 512)
        acc[:, cols] = jnp.dot(n_a[...], wo_own[:, cols], preferred_element_type=F32)
    gain_b[pl.ds(0, NH), :] = gain_ref[pl.ds(g * NH, NH), :]

    send_wo.wait_recv()
    for copy in (*send_x, send_wo, send_k, send_q):
        copy.wait_send()
    for n, first in ((0, 1), (1, 0)):
        kv = (kv_a, kv_b)[n]
        span = pl.ds(0, (PLANE - first) * SL)
        remote(kv.at[span], kv.at[span], s1_sem.at[n], q1_sem.at[n], partner).wait_send()
        tot = (t2a, t2b)[n]
        for k in range(1, NZ):
            @pl.when(z + k < NZ)
            def _():
                remote(tot, tot, s2_sem.at[n, k], q2_sem.at[n, k], partner).wait_send()

    prefix_wait(pfb, 1)
    span = pl.ds(0, (PLANE - 1) * SL)
    for n in range(2):
        remote(kv_a.at[span], kv_a.at[span], s3_sem.at[n], q3_sem.at[n], partner).wait_send()


def out_kernel(acc, y_b, qkv_r, pfb, gain_b, wo_oth, out_hbm, n_b, out_v, st_sem):
    finish(qkv_r, y_b, pfb, gain_b, 0, n_b)
    copies = []
    start = 0
    for n, width in enumerate(WIDTHS):
        cols = pl.ds(start, width)
        mixed = acc[:, cols] + jnp.dot(n_b[...], wo_oth[:, cols], preferred_element_type=F32)
        out_v[:, cols] = mixed.astype(BF16)
        copies.append(pltpu.make_async_copy(out_v.at[:, cols], out_hbm.at[0, :, cols], st_sem.at[n]))
        copies[-1].start()
        start += width
    for copy in copies:
        copy.wait()


def body(tokens, w_qkv, w_out, gain):
    w = jnp.transpose(w_qkv, (1, 0, 2))
    any_ = pl.BlockSpec(memory_space=pl.ANY)
    vm = pltpu.VMEM
    dma = pltpu.SemaphoreType.DMA
    scratch = [
        vm((T, D), BF16), vm((T, D), BF16), vm((3, D, HC), BF16), vm((HC, D), BF16), vm((2 * NH, HD), F32),
        vm((T, 3 * HC), BF16), vm((T, 3 * HC), BF16),
        vm((HC, HD), BF16), vm((HC, HD), BF16),
        vm((PLANE, SL, HD), BF16), vm((PLANE, SL, HD), BF16),
        vm((SL, HD), BF16), vm((SL, HD), BF16),
        vm((NZ, SL, HD), BF16), vm((NZ, SL, HD), BF16),
        vm((PLANE, SL, HD), BF16), vm((PLANE, SL, HD), BF16),
        vm((HC, HD), BF16), vm((HC, HD), F32),
        vm((T, HC), F32), vm((T, HC), BF16),
        dma((7,)), dma((7,)), dma((7,)),
        dma((2,)), dma((2,)), dma((2, NZ)), dma((2, NZ)), dma((2,)), dma((2,)),
        pltpu.SemaphoreType.REGULAR((4,)),
    ]
    whole = pl.BlockSpec(memory_space=pltpu.VMEM)
    late = pl.pallas_call(
        kernel,
        out_shape=[
            vm((T, D), F32), vm((T, HC), F32), vm((T, 3 * HC), BF16), vm((HC, HD), BF16),
            vm((2 * NH, HD), F32), vm((HC, D), BF16),
        ],
        in_specs=[any_] * 4,
        out_specs=[whole] * 6,
        scratch_shapes=scratch,
        compiler_params=pltpu.CompilerParams(
            collective_id=0, has_side_effects=True, vmem_limit_bytes=32 * 1024 * 1024
        ),
        cost_estimate=pl.CostEstimate(flops=9_000_000_000, bytes_accessed=12_000_000, transcendentals=1_600_000),
    )(*(pltpu.with_memory_space_constraint(a, pltpu.HBM) for a in (tokens, w, w_out, gain.reshape(2 * NH, HD))))
    return pl.pallas_call(
        out_kernel,
        out_shape=jax.ShapeDtypeStruct((1, T, D), BF16),
        in_specs=[whole] * 6,
        out_specs=any_,
        scratch_shapes=[vm((T, HC), BF16), vm((T, D), BF16), dma((len(WIDTHS),))],
        compiler_params=pltpu.CompilerParams(vmem_limit_bytes=16 * 1024 * 1024),
        cost_estimate=pl.CostEstimate(flops=1_000_000_000, bytes_accessed=2_000_000, transcendentals=0),
    )(*late)


def solution(mesh):
    in_specs = (P("fsdp", "ctx", None), P(None, None, "fsdp"), P("fsdp", None), P())
    out_specs = P("fsdp", "ctx", None)
    return jax.shard_map(body, mesh=mesh, in_specs=in_specs, out_specs=out_specs, check_vma=False)
```

```python
import jax
import jax.numpy as jnp
from jax import lax
from jax.experimental import pallas as pl
from jax.experimental.pallas import tpu as pltpu
from jax.sharding import PartitionSpec as P

HD = 128
T = 512
D = 2048
NH = 4
HC = NH * HD
PLANE = 16
NZ = 8
SL = HC // PLANE
F32 = jnp.float32
BF16 = jnp.bfloat16
MESH = pl.DeviceIdType.MESH
WIDTHS = (512, 512, 512, 256, 256)
SOON = 5
FAR = sorted(((dx, dy) for dx in range(4) for dy in range(4)), key=lambda o: -min(o[0], 4 - o[0]) - min(o[1], 4 - o[1]))


def silu(v):
    half = 0.5 * v
    return half + half * jnp.tanh(half)


def remote(src, dst, send, recv, device):
    return pltpu.make_async_remote_copy(
        src_ref=src, dst_ref=dst, send_sem=send, recv_sem=recv, device_id=device, device_id_type=MESH
    )


def finish(qkv, y, pf, gain, row, dst):
    for h in range(NH):
        cols = pl.ds(h * HD, HD)
        inter = jnp.dot(qkv[:, cols], pf[cols, :], preferred_element_type=F32)
        total = y[:, cols] + inter
        scale = lax.rsqrt(jnp.mean(total * total, axis=-1, keepdims=True) + 1e-06)
        dst[:, cols] = (total * scale * gain[pl.ds(row + h, 1), :]).astype(BF16)


def kernel(
    x_hbm, w_hbm, wo_hbm, gain_hbm,
    acc, y_b, qkv_r, pfb, gain_b, wo_oth,
    x_own, x_oth, w, wo_own, gain_ref,
    qkv_a, qkv_s,
    kv_a, kv_b, r1a, r1b, t2a, t2b, r2a, r2b, o3a, o3b, pfa, kv_sum,
    y_a, n_a,
    ld_sem, ps_sem, pr_sem, s1_sem, q1_sem, s2_sem, q2_sem, s3_sem, q3_sem, in_sem,
):
    f = lax.axis_index("fsdp")
    c = lax.axis_index("ctx")
    z = c // PLANE
    p = lax.rem(c, PLANE)
    base = z * PLANE
    g = 1 - f

    px, py = p // 4, lax.rem(p, 4)

    def chip(k):
        dx, dy = FAR[k]
        return lax.rem(px + dx, 4) * 4 + lax.rem(py + dy, 4)

    def tell(sem, core, plane, spot):
        pl.semaphore_signal(sem, inc=1, device_id=(core, plane * PLANE + spot), device_id_type=MESH)

    def at(dx, dy):
        return lax.rem(px + dx, 4) * 4 + lax.rem(py + dy, 4)

    halves = [pl.ds(0, T // 2), pl.ds(T // 2, T // 2)]
    sources = (
        (x_hbm.at[0, halves[0]], x_own.at[halves[0]]), (w_hbm.at[1], w.at[1]),
        (x_hbm.at[0, halves[1]], x_own.at[halves[1]]), (w_hbm.at[2], w.at[2]),
        (w_hbm.at[0], w.at[0]), (wo_hbm, wo_own), (gain_hbm, gain_ref),
    )
    loads = [pltpu.make_async_copy(src, dst, ld_sem.at[n]) for n, (src, dst) in enumerate(sources)]
    for copy in loads[:4]:
        copy.start()

    near = ((1, 0), (3, 0), (0, 1), (0, 3))
    barrier = pltpu.get_barrier_semaphore()
    tell(barrier, g, z, p)
    for dx, dy in near:
        tell(barrier, f, z, at(dx, dy))
    for k in (4, 3, 5, 2, 6, 1, 7):
        @pl.when(z + k < NZ)
        def _():
            tell(barrier, f, z + k, p)

    partner = (g, c)
    parts = [pl.ds(0, T // 2), pl.ds(T // 2, T // 4), pl.ds(3 * T // 4, T // 4)]
    send_x = [
        remote(x_hbm.at[0, half], x_oth.at[half], ps_sem.at[4 + n], pr_sem.at[4 + n], partner)
        for n, half in enumerate(parts)
    ]
    send_wo = remote(wo_hbm, wo_oth, ps_sem.at[1], pr_sem.at[1], partner)
    send_k = remote(
        qkv_s.at[:, pl.ds(HC, 2 * HC)], qkv_r.at[:, pl.ds(HC, 2 * HC)], ps_sem.at[2], pr_sem.at[2], partner
    )
    send_q = remote(qkv_s.at[:, pl.ds(0, HC)], qkv_r.at[:, pl.ds(0, HC)], ps_sem.at[3], pr_sem.at[3], partner)

    def project(x, which, dst, rows=pl.ds(0, T)):
        part = jnp.dot(x[rows, :], w[which], preferred_element_type=F32)
        dst[rows, pl.ds(which * HC, HC)] = silu(part).astype(BF16)

    def state(qkv, dst, part=pl.ds(0, T), first=True, last=True):
        for h in range(NH):
            key = qkv[part, pl.ds(HC + h * HD, HD)]
            val = qkv[part, pl.ds(2 * HC + h * HD, HD)]
            kv = lax.dot_general(key, val, (((0,), (0,)), ((), ())), preferred_element_type=F32)
            head = pl.ds(h * HD, HD)
            if not first:
                kv = kv + kv_sum[head, :]
            if last:
                dst[head, :] = kv.astype(BF16)
            else:
                kv_sum[head, :] = kv

    def rows(i):
        return pl.ds(pl.multiple_of(i * SL, SL), SL)

    def scatter_start(kv, got, core, n, first):
        for k in range(PLANE - first):
            j = chip(k)
            remote(kv.at[rows(j)], got.at[p], s1_sem.at[n], q1_sem.at[n], (core, base + j)).start()

    def scatter_wait(kv, got, n, first):
        m = PLANE - first
        remote(kv.at[pl.ds(0, m * SL)], kv.at[pl.ds(0, m * SL)], s1_sem.at[n], q1_sem.at[n], partner).wait_recv()

    def totals_start(got, tot, r2, n):
        total = got[0].astype(F32)
        for i in range(1, PLANE):
            total = total + got[i].astype(F32)
        tot[...] = total.astype(BF16)
        for k in (4, 3, 5, 2, 6, 1, 7):
            @pl.when(z + k < NZ)
            def _():
                remote(
                    tot, r2.at[z], s2_sem.at[n, k], q2_sem.at[n, z], (f, (z + k) * PLANE + p)
                ).start()

    def prefix_start(got, tot, r2, o3, pf, n):
        def add(i, total):
            remote(tot, r2.at[i], s2_sem.at[n, 0], q2_sem.at[n, i], partner).wait_recv()
            return total + r2[i].astype(F32)

        total = lax.fori_loop(0, z, add, jnp.zeros((SL, HD), F32))
        for i in range(PLANE):
            o3[i] = total.astype(BF16)
            if i < PLANE - 1:
                total = total + got[i].astype(F32)
        for k in range(PLANE - 1):
            j = chip(k)
            remote(o3.at[j], pf.at[rows(p)], s3_sem.at[n], q3_sem.at[n], (f, base + j)).start()
        pf[rows(p), :] = o3[p]

    def prefix_wait(pf, n):
        m = PLANE - 1
        remote(pf.at[pl.ds(0, m * SL)], pf.at[pl.ds(0, m * SL)], s3_sem.at[n], q3_sem.at[n], partner).wait_recv()

    half = T // 2
    tri = lax.broadcasted_iota(jnp.int32, (half, half), 0) >= lax.broadcasted_iota(jnp.int32, (half, half), 1)

    def intra(qkv, y):
        nt = (((1,), (1,)), ((), ()))
        for h in range(NH):
            qc, kc, vc = (pl.ds(n * HC + h * HD, HD) for n in range(3))
            lo, hi = pl.ds(0, half), pl.ds(half, half)
            q0, q1 = qkv[lo, qc], qkv[hi, qc]
            k0, k1 = qkv[lo, kc], qkv[hi, kc]
            v0, v1 = qkv[lo, vc], qkv[hi, vc]
            s00 = lax.dot_general(q0, k0, nt, preferred_element_type=F32)
            s10 = lax.dot_general(q1, k0, nt, preferred_element_type=F32)
            s11 = lax.dot_general(q1, k1, nt, preferred_element_type=F32)
            s00 = jnp.where(tri, s00, 0.0).astype(BF16)
            s11 = jnp.where(tri, s11, 0.0).astype(BF16)
            s10 = s10.astype(BF16)
            yc = pl.ds(h * HD, HD)
            y[lo, yc] = jnp.dot(s00, v0, preferred_element_type=F32)
            y[hi, yc] = jnp.dot(s10, v0, preferred_element_type=F32) + jnp.dot(s11, v1, preferred_element_type=F32)

    pl.semaphore_wait(barrier, 5 + z)
    for copy in (*send_x, *loads[4:]):
        copy.start()
    tell(in_sem.at[0], g, z, p)
    for dx, dy in near:
        tell(in_sem.at[0], f, z, at(dx, dy))
    for k in (4, 3, 5, 2, 6, 1, 7):
        @pl.when(z - k >= 0)
        def _():
            tell(in_sem.at[3], f, z - k, p)

    for n in range(2):
        loads[n].wait()
        if n:
            project(x_own, 1, qkv_a, halves[0])
    loads[2].wait()
    project(x_own, 1, qkv_a, halves[1])
    pl.semaphore_wait(in_sem.at[0], 5)
    tell(in_sem.at[1], f, z, at(2, 0))
    tell(in_sem.at[1], f, z, at(0, 2))
    tell(in_sem.at[1], g, z, p)
    loads[3].wait()
    project(x_own, 2, qkv_a)
    state(qkv_a, kv_a)
    pl.semaphore_wait(in_sem.at[1], 3)
    tell(in_sem.at[2], g, z, p)
    scatter_start(kv_a, r1a, f, 0, 1)
    r1a[p] = kv_a[rows(p), :]

    for n, (copy, part) in enumerate(zip(send_x, parts)):
        copy.wait_recv()
        project(x_oth, 1, qkv_s, part)
        project(x_oth, 2, qkv_s, part)
        state(qkv_s, kv_b, part, n == 0, n == 2)
    pl.semaphore_wait(in_sem.at[2], 1)
    scatter_start(kv_b, r1b, g, 1, 0)
    send_k.start()
    loads[4].wait()
    project(x_oth, 0, qkv_s)
    send_q.start()
    scatter_wait(kv_a, r1a, 0, 1)

    @pl.when(z < NZ - 1)
    def _():
        pl.semaphore_wait(in_sem.at[3], NZ - 1 - z)

    totals_start(r1a, t2a, r2a, 0)
    project(x_own, 0, qkv_a)
    send_wo.start()

    @pl.when(z < SOON)
    def _():
        prefix_start(r1a, t2a, r2a, o3a, pfa, 0)

    scatter_wait(kv_b, r1b, 1, 0)
    totals_start(r1b, t2b, r2b, 1)

    @pl.when(z < SOON)
    def _():
        prefix_start(r1b, t2b, r2b, o3b, pfb, 1)

    intra(qkv_a, y_a)

    @pl.when(z >= SOON)
    def _():
        prefix_start(r1a, t2a, r2a, o3a, pfa, 0)

    send_k.wait_recv()
    send_q.wait_recv()

    @pl.when(z >= SOON)
    def _():
        prefix_start(r1b, t2b, r2b, o3b, pfb, 1)

    intra(qkv_r, y_b)
    prefix_wait(pfa, 0)
    loads[6].wait()
    finish(qkv_a, y_a, pfa, gain_ref, f * NH, n_a)
    loads[5].wait()

    for i in range(4):
        cols = pl.ds(i * 512, 512)
        acc[:, cols] = jnp.dot(n_a[...], wo_own[:, cols], preferred_element_type=F32)
    gain_b[pl.ds(0, NH), :] = gain_ref[pl.ds(g * NH, NH), :]

    send_wo.wait_recv()
    for copy in (*send_x, send_wo, send_k, send_q):
        copy.wait_send()
    for n, first in ((0, 1), (1, 0)):
        kv = (kv_a, kv_b)[n]
        span = pl.ds(0, (PLANE - first) * SL)
        remote(kv.at[span], kv.at[span], s1_sem.at[n], q1_sem.at[n], partner).wait_send()
        tot = (t2a, t2b)[n]
        for k in range(1, NZ):
            @pl.when(z + k < NZ)
            def _():
                remote(tot, tot, s2_sem.at[n, k], q2_sem.at[n, k], partner).wait_send()

    prefix_wait(pfb, 1)
    span = pl.ds(0, (PLANE - 1) * SL)
    for n in range(2):
        remote(kv_a.at[span], kv_a.at[span], s3_sem.at[n], q3_sem.at[n], partner).wait_send()


def out_kernel(acc, y_b, qkv_r, pfb, gain_b, wo_oth, out_hbm, n_b, out_v, st_sem):
    finish(qkv_r, y_b, pfb, gain_b, 0, n_b)
    copies = []
    start = 0
    for n, width in enumerate(WIDTHS):
        cols = pl.ds(start, width)
        mixed = acc[:, cols] + jnp.dot(n_b[...], wo_oth[:, cols], preferred_element_type=F32)
        out_v[:, cols] = mixed.astype(BF16)
        copies.append(pltpu.make_async_copy(out_v.at[:, cols], out_hbm.at[0, :, cols], st_sem.at[n]))
        copies[-1].start()
        start += width
    for copy in copies:
        copy.wait()


def body(tokens, w_qkv, w_out, gain):
    w = jnp.transpose(w_qkv, (1, 0, 2))
    any_ = pl.BlockSpec(memory_space=pl.ANY)
    vm = pltpu.VMEM
    dma = pltpu.SemaphoreType.DMA
    scratch = [
        vm((T, D), BF16), vm((T, D), BF16), vm((3, D, HC), BF16), vm((HC, D), BF16), vm((2 * NH, HD), F32),
        vm((T, 3 * HC), BF16), vm((T, 3 * HC), BF16),
        vm((HC, HD), BF16), vm((HC, HD), BF16),
        vm((PLANE, SL, HD), BF16), vm((PLANE, SL, HD), BF16),
        vm((SL, HD), BF16), vm((SL, HD), BF16),
        vm((NZ, SL, HD), BF16), vm((NZ, SL, HD), BF16),
        vm((PLANE, SL, HD), BF16), vm((PLANE, SL, HD), BF16),
        vm((HC, HD), BF16), vm((HC, HD), F32),
        vm((T, HC), F32), vm((T, HC), BF16),
        dma((7,)), dma((7,)), dma((7,)),
        dma((2,)), dma((2,)), dma((2, NZ)), dma((2, NZ)), dma((2,)), dma((2,)),
        pltpu.SemaphoreType.REGULAR((4,)),
    ]
    whole = pl.BlockSpec(memory_space=pltpu.VMEM)
    late = pl.pallas_call(
        kernel,
        out_shape=[
            vm((T, D), F32), vm((T, HC), F32), vm((T, 3 * HC), BF16), vm((HC, HD), BF16),
            vm((2 * NH, HD), F32), vm((HC, D), BF16),
        ],
        in_specs=[any_] * 4,
        out_specs=[whole] * 6,
        scratch_shapes=scratch,
        compiler_params=pltpu.CompilerParams(
            collective_id=0, has_side_effects=True, vmem_limit_bytes=32 * 1024 * 1024
        ),
        cost_estimate=pl.CostEstimate(flops=9_000_000_000, bytes_accessed=12_000_000, transcendentals=1_600_000),
    )(*(pltpu.with_memory_space_constraint(a, pltpu.HBM) for a in (tokens, w, w_out, gain.reshape(2 * NH, HD))))
    return pl.pallas_call(
        out_kernel,
        out_shape=jax.ShapeDtypeStruct((1, T, D), BF16),
        in_specs=[whole] * 6,
        out_specs=any_,
        scratch_shapes=[vm((T, HC), BF16), vm((T, D), BF16), dma((len(WIDTHS),))],
        compiler_params=pltpu.CompilerParams(vmem_limit_bytes=16 * 1024 * 1024),
        cost_estimate=pl.CostEstimate(flops=1_000_000_000, bytes_accessed=2_000_000, transcendentals=0),
    )(*late)


def solution(mesh):
    in_specs = (P("fsdp", "ctx", None), P(None, None, "fsdp"), P("fsdp", None), P())
    out_specs = P("fsdp", "ctx", None)
    return jax.shard_map(body, mesh=mesh, in_specs=in_specs, out_specs=out_specs, check_vma=False)
```

```python
import jax
import jax.numpy as jnp
from jax import lax
from jax.experimental import pallas as pl
from jax.experimental.pallas import tpu as pltpu
from jax.sharding import PartitionSpec as P

HD = 128
T = 512
D = 2048
NH = 4
HC = NH * HD
PLANE = 16
NZ = 8
SL = HC // PLANE
F32 = jnp.float32
BF16 = jnp.bfloat16
MESH = pl.DeviceIdType.MESH
WIDTHS = (512, 512, 512, 256, 256)
SOON = 5
FAR = sorted(((dx, dy) for dx in range(4) for dy in range(4)), key=lambda o: -min(o[0], 4 - o[0]) - min(o[1], 4 - o[1]))


def silu(v):
    half = 0.5 * v
    return half + half * jnp.tanh(half)


def remote(src, dst, send, recv, device):
    return pltpu.make_async_remote_copy(
        src_ref=src, dst_ref=dst, send_sem=send, recv_sem=recv, device_id=device, device_id_type=MESH
    )


def finish(qkv, y, pf, gain, row, dst):
    for h in range(NH):
        cols = pl.ds(h * HD, HD)
        inter = jnp.dot(qkv[:, cols], pf[cols, :], preferred_element_type=F32)
        total = y[:, cols] + inter
        scale = lax.rsqrt(jnp.mean(total * total, axis=-1, keepdims=True) + 1e-06)
        dst[:, cols] = (total * scale * gain[pl.ds(row + h, 1), :]).astype(BF16)


def kernel(
    x_hbm, w_hbm, wo_hbm, gain_hbm,
    acc, y_b, qkv_r, pfb, gain_b, wo_oth,
    x_own, x_oth, w, wo_own, gain_ref,
    qkv_a, qkv_s,
    kv_a, kv_b, r1a, r1b, t2a, t2b, r2a, r2b, o3a, o3b, pfa, kv_sum, before,
    y_a, n_a,
    ld_sem, ps_sem, pr_sem, s1_sem, q1_sem, s2_sem, q2_sem, s3_sem, q3_sem, in_sem,
):
    f = lax.axis_index("fsdp")
    c = lax.axis_index("ctx")
    z = c // PLANE
    p = lax.rem(c, PLANE)
    base = z * PLANE
    g = 1 - f

    px, py = p // 4, lax.rem(p, 4)

    def chip(k):
        dx, dy = FAR[k]
        return lax.rem(px + dx, 4) * 4 + lax.rem(py + dy, 4)

    def tell(sem, core, plane, spot):
        pl.semaphore_signal(sem, inc=1, device_id=(core, plane * PLANE + spot), device_id_type=MESH)

    def at(dx, dy):
        return lax.rem(px + dx, 4) * 4 + lax.rem(py + dy, 4)

    halves = [pl.ds(0, T // 2), pl.ds(T // 2, T // 2)]
    sources = (
        (x_hbm.at[0, halves[0]], x_own.at[halves[0]]), (w_hbm.at[1], w.at[1]),
        (x_hbm.at[0, halves[1]], x_own.at[halves[1]]), (w_hbm.at[2], w.at[2]),
        (w_hbm.at[0], w.at[0]), (wo_hbm, wo_own), (gain_hbm, gain_ref),
    )
    loads = [pltpu.make_async_copy(src, dst, ld_sem.at[n]) for n, (src, dst) in enumerate(sources)]
    for copy in loads:
        copy.start()

    near = ((1, 0), (3, 0), (0, 1), (0, 3))
    barrier = pltpu.get_barrier_semaphore()
    tell(barrier, g, z, p)
    for dx, dy in near:
        tell(barrier, f, z, at(dx, dy))
    for k in (4, 3, 5, 2, 6, 1, 7):
        @pl.when(z + k < NZ)
        def _():
            tell(barrier, f, z + k, p)

    partner = (g, c)
    parts = [pl.ds(0, 3 * T // 4), pl.ds(3 * T // 4, T // 4)]
    send_x = [
        remote(x_hbm.at[0, half], x_oth.at[half], ps_sem.at[4 + n], pr_sem.at[4 + n], partner)
        for n, half in enumerate(parts)
    ]
    send_wo = remote(wo_hbm, wo_oth, ps_sem.at[1], pr_sem.at[1], partner)
    send_k = remote(
        qkv_s.at[:, pl.ds(HC, 2 * HC)], qkv_r.at[:, pl.ds(HC, 2 * HC)], ps_sem.at[2], pr_sem.at[2], partner
    )
    send_q = remote(qkv_s.at[:, pl.ds(0, HC)], qkv_r.at[:, pl.ds(0, HC)], ps_sem.at[3], pr_sem.at[3], partner)

    def project(x, which, dst, rows=pl.ds(0, T)):
        part = jnp.dot(x[rows, :], w[which], preferred_element_type=F32)
        dst[rows, pl.ds(which * HC, HC)] = silu(part).astype(BF16)

    def state(qkv, dst, part=pl.ds(0, T), first=True, last=True):
        for h in range(NH):
            key = qkv[part, pl.ds(HC + h * HD, HD)]
            val = qkv[part, pl.ds(2 * HC + h * HD, HD)]
            kv = lax.dot_general(key, val, (((0,), (0,)), ((), ())), preferred_element_type=F32)
            head = pl.ds(h * HD, HD)
            if not first:
                kv = kv + kv_sum[head, :]
            if last:
                dst[head, :] = kv.astype(BF16)
            else:
                kv_sum[head, :] = kv

    def rows(i):
        return pl.ds(pl.multiple_of(i * SL, SL), SL)

    def scatter_start(kv, got, core, n, first):
        for k in range(PLANE - first):
            j = chip(k)
            remote(kv.at[rows(j)], got.at[p], s1_sem.at[n], q1_sem.at[n], (core, base + j)).start()

    def scatter_wait(kv, got, n, first):
        m = PLANE - first
        remote(kv.at[pl.ds(0, m * SL)], kv.at[pl.ds(0, m * SL)], s1_sem.at[n], q1_sem.at[n], partner).wait_recv()

    def totals_start(got, tot, r2, n):
        total = got[0].astype(F32)
        before[n, 0] = jnp.zeros((SL, HD), F32)
        for i in range(1, PLANE):
            before[n, i] = total
            total = total + got[i].astype(F32)
        tot[...] = total.astype(BF16)
        for k in (4, 3, 5, 2, 6, 1, 7):
            @pl.when(z + k < NZ)
            def _():
                remote(
                    tot, r2.at[z], s2_sem.at[n, k], q2_sem.at[n, z], (f, (z + k) * PLANE + p)
                ).start()

    def prefix_start(got, tot, r2, o3, pf, n):
        def add(i, total):
            remote(tot, r2.at[i], s2_sem.at[n, 0], q2_sem.at[n, i], partner).wait_recv()
            return total + r2[i].astype(F32)

        total = lax.fori_loop(0, z, add, jnp.zeros((SL, HD), F32))
        for k in range(PLANE - 1):
            j = chip(k)
            o3[j] = (total + before[n, j]).astype(BF16)
            remote(o3.at[j], pf.at[rows(p)], s3_sem.at[n], q3_sem.at[n], (f, base + j)).start()
        pf[rows(p), :] = (total + before[n, p]).astype(BF16)

    def prefix_wait(pf, n):
        m = PLANE - 1
        remote(pf.at[pl.ds(0, m * SL)], pf.at[pl.ds(0, m * SL)], s3_sem.at[n], q3_sem.at[n], partner).wait_recv()

    half = T // 2
    tri = lax.broadcasted_iota(jnp.int32, (half, half), 0) >= lax.broadcasted_iota(jnp.int32, (half, half), 1)

    def intra(qkv, y):
        nt = (((1,), (1,)), ((), ()))
        for h in range(NH):
            qc, kc, vc = (pl.ds(n * HC + h * HD, HD) for n in range(3))
            lo, hi = pl.ds(0, half), pl.ds(half, half)
            q0, q1 = qkv[lo, qc], qkv[hi, qc]
            k0, k1 = qkv[lo, kc], qkv[hi, kc]
            v0, v1 = qkv[lo, vc], qkv[hi, vc]
            s00 = lax.dot_general(q0, k0, nt, preferred_element_type=F32)
            s10 = lax.dot_general(q1, k0, nt, preferred_element_type=F32)
            s11 = lax.dot_general(q1, k1, nt, preferred_element_type=F32)
            s00 = jnp.where(tri, s00, 0.0).astype(BF16)
            s11 = jnp.where(tri, s11, 0.0).astype(BF16)
            s10 = s10.astype(BF16)
            yc = pl.ds(h * HD, HD)
            y[lo, yc] = jnp.dot(s00, v0, preferred_element_type=F32)
            y[hi, yc] = jnp.dot(s10, v0, preferred_element_type=F32) + jnp.dot(s11, v1, preferred_element_type=F32)

    pl.semaphore_wait(barrier, 5 + z)
    for copy in send_x:
        copy.start()
    tell(in_sem.at[0], g, z, p)
    for dx, dy in near:
        tell(in_sem.at[0], f, z, at(dx, dy))
    for k in (4, 3, 5, 2, 6, 1, 7):
        @pl.when(z - k >= 0)
        def _():
            tell(in_sem.at[3], f, z - k, p)

    for n in range(2):
        loads[n].wait()
        if n:
            project(x_own, 1, qkv_a, halves[0])
    loads[2].wait()
    project(x_own, 1, qkv_a, halves[1])
    pl.semaphore_wait(in_sem.at[0], 5)
    tell(in_sem.at[1], f, z, at(2, 0))
    tell(in_sem.at[1], f, z, at(0, 2))
    tell(in_sem.at[1], g, z, p)
    loads[3].wait()
    project(x_own, 2, qkv_a)
    state(qkv_a, kv_a)
    pl.semaphore_wait(in_sem.at[1], 3)
    tell(in_sem.at[2], g, z, p)
    scatter_start(kv_a, r1a, f, 0, 1)
    r1a[p] = kv_a[rows(p), :]

    for n, (copy, part) in enumerate(zip(send_x, parts)):
        copy.wait_recv()
        project(x_oth, 1, qkv_s, part)
        project(x_oth, 2, qkv_s, part)
        state(qkv_s, kv_b, part, n == 0, n == 1)
    pl.semaphore_wait(in_sem.at[2], 1)
    scatter_start(kv_b, r1b, g, 1, 0)
    send_k.start()
    loads[4].wait()
    project(x_oth, 0, qkv_s)
    send_q.start()
    scatter_wait(kv_a, r1a, 0, 1)

    @pl.when(z < NZ - 1)
    def _():
        pl.semaphore_wait(in_sem.at[3], NZ - 1 - z)

    totals_start(r1a, t2a, r2a, 0)
    project(x_own, 0, qkv_a)
    send_wo.start()

    @pl.when(z < SOON)
    def _():
        prefix_start(r1a, t2a, r2a, o3a, pfa, 0)

    scatter_wait(kv_b, r1b, 1, 0)
    totals_start(r1b, t2b, r2b, 1)

    @pl.when(z < SOON)
    def _():
        prefix_start(r1b, t2b, r2b, o3b, pfb, 1)

    intra(qkv_a, y_a)

    @pl.when(z >= SOON)
    def _():
        prefix_start(r1a, t2a, r2a, o3a, pfa, 0)

    send_k.wait_recv()
    send_q.wait_recv()

    @pl.when(z >= SOON)
    def _():
        prefix_start(r1b, t2b, r2b, o3b, pfb, 1)

    intra(qkv_r, y_b)
    prefix_wait(pfa, 0)
    loads[6].wait()
    finish(qkv_a, y_a, pfa, gain_ref, f * NH, n_a)
    loads[5].wait()

    for i in range(4):
        cols = pl.ds(i * 512, 512)
        acc[:, cols] = jnp.dot(n_a[...], wo_own[:, cols], preferred_element_type=F32)
    gain_b[pl.ds(0, NH), :] = gain_ref[pl.ds(g * NH, NH), :]

    send_wo.wait_recv()
    for copy in (*send_x, send_wo, send_k, send_q):
        copy.wait_send()
    for n, first in ((0, 1), (1, 0)):
        kv = (kv_a, kv_b)[n]
        span = pl.ds(0, (PLANE - first) * SL)
        remote(kv.at[span], kv.at[span], s1_sem.at[n], q1_sem.at[n], partner).wait_send()
        tot = (t2a, t2b)[n]
        for k in range(1, NZ):
            @pl.when(z + k < NZ)
            def _():
                remote(tot, tot, s2_sem.at[n, k], q2_sem.at[n, k], partner).wait_send()

    prefix_wait(pfb, 1)
    span = pl.ds(0, (PLANE - 1) * SL)
    for n in range(2):
        remote(kv_a.at[span], kv_a.at[span], s3_sem.at[n], q3_sem.at[n], partner).wait_send()


def out_kernel(acc, y_b, qkv_r, pfb, gain_b, wo_oth, out_hbm, n_b, out_v, st_sem):
    finish(qkv_r, y_b, pfb, gain_b, 0, n_b)
    copies = []
    start = 0
    for n, width in enumerate(WIDTHS):
        cols = pl.ds(start, width)
        mixed = acc[:, cols] + jnp.dot(n_b[...], wo_oth[:, cols], preferred_element_type=F32)
        out_v[:, cols] = mixed.astype(BF16)
        copies.append(pltpu.make_async_copy(out_v.at[:, cols], out_hbm.at[0, :, cols], st_sem.at[n]))
        copies[-1].start()
        start += width
    for copy in copies:
        copy.wait()


def body(tokens, w_qkv, w_out, gain):
    w = jnp.transpose(w_qkv, (1, 0, 2))
    any_ = pl.BlockSpec(memory_space=pl.ANY)
    vm = pltpu.VMEM
    dma = pltpu.SemaphoreType.DMA
    scratch = [
        vm((T, D), BF16), vm((T, D), BF16), vm((3, D, HC), BF16), vm((HC, D), BF16), vm((2 * NH, HD), F32),
        vm((T, 3 * HC), BF16), vm((T, 3 * HC), BF16),
        vm((HC, HD), BF16), vm((HC, HD), BF16),
        vm((PLANE, SL, HD), BF16), vm((PLANE, SL, HD), BF16),
        vm((SL, HD), BF16), vm((SL, HD), BF16),
        vm((NZ, SL, HD), BF16), vm((NZ, SL, HD), BF16),
        vm((PLANE, SL, HD), BF16), vm((PLANE, SL, HD), BF16),
        vm((HC, HD), BF16), vm((HC, HD), F32), vm((2, PLANE, SL, HD), F32),
        vm((T, HC), F32), vm((T, HC), BF16),
        dma((7,)), dma((7,)), dma((7,)),
        dma((2,)), dma((2,)), dma((2, NZ)), dma((2, NZ)), dma((2,)), dma((2,)),
        pltpu.SemaphoreType.REGULAR((4,)),
    ]
    whole = pl.BlockSpec(memory_space=pltpu.VMEM)
    late = pl.pallas_call(
        kernel,
        out_shape=[
            vm((T, D), F32), vm((T, HC), F32), vm((T, 3 * HC), BF16), vm((HC, HD), BF16),
            vm((2 * NH, HD), F32), vm((HC, D), BF16),
        ],
        in_specs=[any_] * 4,
        out_specs=[whole] * 6,
        scratch_shapes=scratch,
        compiler_params=pltpu.CompilerParams(
            collective_id=0, has_side_effects=True, vmem_limit_bytes=32 * 1024 * 1024
        ),
        cost_estimate=pl.CostEstimate(flops=9_000_000_000, bytes_accessed=12_000_000, transcendentals=1_600_000),
    )(*(pltpu.with_memory_space_constraint(a, pltpu.HBM) for a in (tokens, w, w_out, gain.reshape(2 * NH, HD))))
    return pl.pallas_call(
        out_kernel,
        out_shape=jax.ShapeDtypeStruct((1, T, D), BF16),
        in_specs=[whole] * 6,
        out_specs=any_,
        scratch_shapes=[vm((T, HC), BF16), vm((T, D), BF16), dma((len(WIDTHS),))],
        compiler_params=pltpu.CompilerParams(vmem_limit_bytes=16 * 1024 * 1024),
        cost_estimate=pl.CostEstimate(flops=1_000_000_000, bytes_accessed=2_000_000, transcendentals=0),
    )(*late)


def solution(mesh):
    in_specs = (P("fsdp", "ctx", None), P(None, None, "fsdp"), P("fsdp", None), P())
    out_specs = P("fsdp", "ctx", None)
    return jax.shard_map(body, mesh=mesh, in_specs=in_specs, out_specs=out_specs, check_vma=False)
```
